512 devices in a mesh: group: 64 (over z, x), local: 8 (over y, core).
Axes of the slice: x: 4, y: 4, z: 16, core: 2. Of those that a mesh axis runs over, the one named last changes fastest.
Arguments:
- layer_input: bfloat16 [8192, 3584], P('group', 'local'), may hold values from -6 to 6
- out_grad: bfloat16 [8192, 3584], P('group', 'local'), may hold values from -6 to 6
- expert_ids: int32 [8192, 2], P('group'), may hold values from 0 to 63, all different within a row; in each aligned block of 128 rows (0 to 127, 128 to 255, ...) at most 8 rows name the same one
- gate_probs: float32 [8192, 2], P('group'), may hold values from 0.05 to 1
- w_gate: bfloat16 [64, 3584, 1024], P('group', None, 'local'), may hold values from -0.09375 to 0.09375
- w_up: bfloat16 [64, 3584, 1024], P('group', None, 'local'), may hold values from -0.09375 to 0.09375
- w_down: bfloat16 [64, 1024, 3584], P('group', 'local'), may hold values from -0.1875 to 0.1875
Outputs:
- input_grad: bfloat16 [8192, 3584], P('group', 'local')
The draws below stay inside these ranges and needn't reach their ends.
Inputs may be any that keep to these rules, and one draw needn't show every extreme that they name: `expert_ids`: each token names 2 different experts. Among the 128 tokens held by one index of group, at most 8 name any one expert, a bound that some block reaches of them.
All inputs are finite; a program needn't handle non-finite values.
Results may differ from the reference program's by a relative error of at most 0.019.
Values may be sent and summed in bfloat16 or wider, within the bound.
No kernel may reach another device: no remote copies, remote signals or barrier semaphores. Data moves between devices by JAX's collectives and lax.ppermute only.
A program may use at most 64 MiB of HBM per device.

```python
import math
import jax
import jax.numpy as jnp
import numpy as np
from jax import lax

D = 3584
FF = 1024
TOK_GRP = 128
TOP = 2
EXPERTS = 64
CAP = 8
TOKENS = 8192
N_GROUP = 64
N_LOCAL = 8


def shard_levels(rng, dims, split, low, largest):
    loudness, own = 1.0, jax.random.fold_in(rng, 6)
    for axis_at, shards_of in split:
        steps = jnp.exp(jax.random.uniform(jax.random.fold_in(own, axis_at), (shards_of,), jnp.float32, low / len(split), largest / len(split)))
        loudness = loudness * jnp.repeat(steps, dims[axis_at] // shards_of).reshape([-1 if axis == axis_at else 1 for axis in range(len(dims))])
    return loudness


def assign_block(stream_key, own, number, rows, count, top, most, lean):
    ranking = jax.random.permutation(stream_key, count)
    heavy_load, ordinary = portions_of(count, rows * top, most, lean, True), portions_of(count, rows * top, most, lean, False)
    places = jnp.arange(count)

    def named(lengths, rotation):
        used = int((lengths > 0).sum())
        fixed = max(1, used // 4)
        shifted = fixed + (places - fixed + rotation * (used - fixed)) % max(1, count - fixed)
        return jnp.zeros((count,), jnp.int32).at[ranking[jnp.where(places < fixed, places, shifted)]].set(jnp.asarray(lengths, jnp.int32))

    lengths = jnp.where(number % 4 == 0, named(heavy_load, number // 4), named(ordinary, number - number // 4 - 1))
    mixed = jax.random.permutation(jax.random.fold_in(own, 3), count)
    source_of, sink = mixed[0:count // 2 * 2:2], mixed[1:count // 2 * 2:2]
    margin = jnp.minimum(lengths[source_of] - 1, most - lengths[sink]) // 2
    margin = jnp.where((source_of == ranking[0]) | (sink == ranking[0]) | (lengths[sink] == 0), 0, jnp.maximum(margin, 0))
    shifted = jax.random.randint(jax.random.fold_in(own, 4), (count // 2,), 0, 1 << 20) % (margin + 1)
    lengths = lengths.at[source_of].add(-shifted).at[sink].add(shifted)
    labels = jnp.searchsorted(jnp.cumsum(lengths), jnp.arange(rows * top), side="right").astype(jnp.int32)
    grid = labels.reshape(top, rows).T
    grid = grid[jax.random.permutation(jax.random.fold_in(own, 1), rows)]
    rotation = jax.random.randint(jax.random.fold_in(own, 2), (rows, 1), 0, top)
    return jnp.take_along_axis(grid, (jnp.arange(top)[None, :] + rotation) % top, axis=1)


def portions_of(amount, total, most, skew, full):
    weights = [(1 << 20) // math.isqrt(rank ** skew) + 1 for rank in range(1, amount + 1)]
    largest = most if full else min(most, max(-(-total // amount), total * weights[0] // sum(weights)))
    least = 1 if total - largest >= amount - 1 else 0
    given, rest = [largest] + [least] * (amount - 1), total - largest - least * (amount - 1)
    while rest > 0:
        free = [i for i in range(1, amount) if given[i] < largest] or [i for i in range(1, amount) if given[i] < most]
        whole, budget = sum([weights[i] for i in free]), rest
        for i in free:
            extra = min(most - given[i], max(1, budget * weights[i] // whole), rest)
            given[i] = given[i] + extra
            rest = rest - extra
    return np.array(given)


def noise(rng, dims, width, most, split=(), kind=jnp.bfloat16):
    level = shard_levels(rng, dims, split, -0.22, 0.18) if split else 1.0
    result = jax.random.normal(rng, dims, jnp.float32) * width * level
    return jnp.minimum(jnp.maximum(result, -most), most).astype(kind)


def setup_inputs(seed: int = 0) -> dict:
    streams_of = jax.random.split(jax.random.key(seed), 8)
    layer_input = noise(streams_of[0], (TOKENS, D), 1.0, 6.0, ((0, 64), (1, 8)))
    out_grad = noise(streams_of[1], (TOKENS, D), 1.0, 6.0, ((0, 64), (1, 8)))
    expert_ids_keys = jax.random.split(jax.random.fold_in(streams_of[2], 1), TOKENS // TOK_GRP)
    expert_ids_turns = jax.random.permutation(jax.random.fold_in(streams_of[2], 3), TOKENS // TOK_GRP)
    expert_ids = jax.vmap(lambda own, number: assign_block(jax.random.fold_in(streams_of[2], 2), own, number, TOK_GRP, EXPERTS, TOP, CAP, 2))(expert_ids_keys, expert_ids_turns).reshape((TOKENS, TOP))
    gate_probs = jnp.clip(jnp.exp(math.log(1.0) - 2.9957323 * jax.random.uniform(streams_of[3], (TOKENS, TOP), jnp.float32) ** shard_levels(streams_of[3], (TOKENS, TOP), ((0, 64),), -0.2, 0.2)), 0.05, 1.0)
    w_gate = noise(streams_of[4], (EXPERTS, D, FF), D ** -0.5, 0.09375, ((0, 64), (2, 8)))
    w_up = noise(streams_of[5], (EXPERTS, D, FF), D ** -0.5, 0.09375, ((0, 64), (2, 8)))
    w_down = noise(streams_of[6], (EXPERTS, FF, D), FF ** -0.5, 0.1875, ((0, 64), (1, 8)))
    return dict(layer_input=layer_input, out_grad=out_grad, expert_ids=expert_ids, gate_probs=gate_probs, w_gate=w_gate, w_up=w_up, w_down=w_down)


def silu_backward(gate_act, up_act, hidden_grad):
    sigmoid_gate = jax.nn.sigmoid(gate_act)
    silu_value = gate_act * sigmoid_gate
    gate_grad = hidden_grad * up_act * sigmoid_gate * (1.0 + gate_act * (1.0 - sigmoid_gate))
    return gate_grad.astype(jnp.bfloat16), (hidden_grad * silu_value).astype(jnp.bfloat16)


def contract_last(left, right):
    return lax.dot_general(left, right, (((1,), (1,)), ((), ())), preferred_element_type=jnp.float32)


def reference(layer_input, out_grad, expert_ids, gate_probs, w_gate, w_up, w_down):
    slot_rows = N_GROUP * CAP
    block_width = FF // N_LOCAL
    flat_ids = expert_ids.reshape(-1).astype(jnp.int32)
    flat_probs = gate_probs.reshape(-1)
    ordering = jnp.argsort(flat_ids, stable=True).astype(jnp.int32)
    matches = (flat_ids[:, None] == jnp.arange(EXPERTS, dtype=jnp.int32)[None, :]).astype(jnp.int32)
    per_expert = jnp.sum(matches, axis=0).astype(jnp.int32)
    firsts = (jnp.cumsum(per_expert) - per_expert).astype(jnp.int32)
    padded_order = jnp.concatenate([ordering, jnp.zeros((slot_rows,), jnp.int32)])

    def one_expert(totals, inputs):
        expert, gate_w, up_w, down_w = inputs
        picked = lax.dynamic_slice(padded_order, (firsts[expert].astype(jnp.int32),), (slot_rows,)).astype(jnp.int32)
        live_rows = jnp.arange(slot_rows, dtype=jnp.int32) < per_expert[expert]
        token_index = (picked // TOP).astype(jnp.int32)
        rows_in = layer_input[token_index]
        rows_grad = out_grad[token_index]
        gate_act = jnp.dot(rows_in, gate_w, preferred_element_type=jnp.float32)
        up_act = jnp.dot(rows_in, up_w, preferred_element_type=jnp.float32)
        hidden_grad = contract_last(rows_grad, down_w)
        gate_grad, up_grad = silu_backward(gate_act, up_act, hidden_grad)
        partial_sum = jnp.zeros((slot_rows, D), jnp.float32)
        for block_id in range(N_LOCAL):
            low_edge = block_id * block_width
            high_edge = low_edge + block_width
            block_term = contract_last(gate_grad[:, low_edge:high_edge], gate_w[:, low_edge:high_edge])
            block_term = block_term + contract_last(up_grad[:, low_edge:high_edge], up_w[:, low_edge:high_edge])
            rounded = lax.optimization_barrier(block_term.astype(jnp.bfloat16))
            partial_sum = partial_sum + rounded.astype(jnp.float32)
        weights = jnp.where(live_rows, flat_probs[picked], jnp.zeros_like(flat_probs[picked]))
        totals = totals.at[token_index].add(partial_sum * weights[:, None])
        return totals, None

    totals, ignored = lax.scan(one_expert, jnp.zeros((TOKENS, D), jnp.float32), (jnp.arange(EXPERTS, dtype=jnp.int32), w_gate, w_up, w_down))
    return totals.astype(jnp.bfloat16)
```

```python
import jax
import jax.numpy as jnp
from jax import lax
from jax.sharding import Mesh, PartitionSpec as P

N_Z, N_X, N_Y, N_C = 16, 4, 4, 2
GROUP = ("z", "x")
LOCAL = ("y", "c")
SLOTS = 4


def dot(left, right, left_dim, right_dim):
    return lax.dot_general(
        left, right, (((left_dim,), (right_dim,)), ((), ())), preferred_element_type=jnp.float32
    )


def shift(value, axis, step, size):
    return lax.ppermute(value, axis, [(i, (i + step) % size) for i in range(size)])


def shards(layer_input, out_grad, expert_ids, gate_probs, w_gate, w_up, w_down):
    bf16 = jnp.bfloat16
    groups = N_Z * N_X
    tokens, width = layer_input.shape
    rows = groups * SLOTS
    chip = N_C * width
    core = lax.axis_index("c")
    here = lax.axis_index("y")

    own = jnp.stack([layer_input.T, out_grad.T])
    both = lax.all_gather(own, "c", axis=1, tiled=True).reshape(2 * chip, tokens)

    first, second = expert_ids[:, 0], expert_ids[:, 1]
    position = jnp.arange(tokens, dtype=jnp.int32)
    before = position[None, :] < position[:, None]

    def rank(ids):
        same = (ids[:, None] == first[None, :]) | (ids[:, None] == second[None, :])
        return jnp.sum((same & before).astype(jnp.int32), axis=1)

    def slot_of(ids):
        place = rank(ids) - SLOTS * core
        return jnp.where((place >= 0) & (place < SLOTS), ids * SLOTS + place, -1)

    slot_ids = jnp.arange(rows, dtype=jnp.int32)
    hit_first = slot_of(first)[None, :] == slot_ids[:, None]
    hit_second = slot_of(second)[None, :] == slot_ids[:, None]
    select = (hit_first | hit_second).astype(bf16)
    weight = jnp.where(hit_first, gate_probs[:, 0][None, :], 0.0) + jnp.where(
        hit_second, gate_probs[:, 1][None, :], 0.0
    )
    weight_high = weight.astype(bf16)
    weight_low = (weight - weight_high.astype(jnp.float32)).astype(bf16)
    weights = jnp.concatenate([weight_high, weight_low], axis=1)

    send = dot(select, both, 1, 1).astype(bf16).reshape(groups, SLOTS, 2 * chip)
    send, w_gate, w_up, w_down = lax.optimization_barrier((send, w_gate, w_up, w_down))
    recv = lax.all_to_all(send, GROUP, split_axis=0, concat_axis=0, tiled=True)

    mats = jnp.stack([w_gate[0], w_up[0], w_down[0].T])

    def part(step):
        return lax.dynamic_slice_in_dim(mats, chip * ((here + step) % N_Y), chip, axis=1)

    blocks = jnp.stack([part(0)] + [shift(part(d), "y", d, N_Y) for d in range(1, N_Y)])
    other = shift(blocks, "c", 1, N_C)
    full = [
        jnp.concatenate([blocks[d], other[d]], axis=2) for d in range(N_Y)
    ]

    recv = recv.reshape(rows, 2 * chip)
    rows_in, rows_grad = recv[:, :chip], recv[:, chip:]

    def partial(d):
        return jnp.stack(
            [dot(rows_in, full[d][0], 1, 0), dot(rows_in, full[d][1], 1, 0), dot(rows_grad, full[d][2], 1, 0)]
        )

    sums = partial(0)
    for d in range(1, N_Y):
        sums = sums + shift(partial(d).astype(bf16), "y", -d, N_Y).astype(jnp.float32)
    gate_act, up_act, hidden_grad = sums[0], sums[1], sums[2]
    sigmoid_gate = jax.nn.sigmoid(gate_act)
    gate_grad = hidden_grad * up_act * sigmoid_gate * (1.0 + gate_act * (1.0 - sigmoid_gate))
    up_grad = hidden_grad * gate_act * sigmoid_gate
    grads = jnp.stack([gate_grad.astype(bf16), up_grad.astype(bf16)])
    back = jnp.zeros((rows, chip), jnp.float32)
    for d in range(N_Y):
        theirs = shift(grads, "y", d, N_Y) if d else grads
        back = back + dot(theirs[0], full[d][0], 1, 1) + dot(theirs[1], full[d][1], 1, 1)

    returned = lax.all_to_all(
        back.astype(bf16).reshape(groups, SLOTS, chip), GROUP, split_axis=0, concat_axis=0, tiled=True
    ).reshape(rows, chip)
    mixed = dot(returned, weights, 0, 0)
    mixed = (mixed[:, :tokens] + mixed[:, tokens:]).reshape(N_C, width, tokens)
    mine = lax.dynamic_index_in_dim(mixed, core, 0, keepdims=False)
    sibling = lax.dynamic_index_in_dim(mixed, 1 - core, 0, keepdims=False)
    result = mine + shift(sibling, "c", 1, N_C)
    return result.astype(bf16).T


def solution(mesh):
    split = Mesh(mesh.devices.reshape(N_Z, N_X, N_Y, N_C), GROUP + LOCAL)
    placed = (
        P(GROUP, LOCAL),
        P(GROUP, LOCAL),
        P(GROUP, None),
        P(GROUP, None),
        P(GROUP, None, LOCAL),
        P(GROUP, None, LOCAL),
        P(GROUP, LOCAL, None),
    )
    return jax.shard_map(
        shards, mesh=split, in_specs=placed, out_specs=P(GROUP, LOCAL), check_vma=False
    )
```

```python
import jax
import jax.numpy as jnp
from jax import lax
from jax.experimental import pallas as pl
from jax.experimental.pallas import tpu as pltpu
from jax.sharding import Mesh, PartitionSpec as P

N_Z, N_X, N_Y, N_C = 16, 4, 4, 2
GROUP = ("z", "x")
LOCAL = ("y", "c")
SLOTS = 4
BF16 = jnp.bfloat16
F32 = jnp.float32


def dot(left, right, left_dim, right_dim):
    return lax.dot_general(
        left, right, (((left_dim,), (right_dim,)), ((), ())), preferred_element_type=F32
    )


def shift(value, axis, step, size):
    return lax.ppermute(value, axis, [(i, (i + step) % size) for i in range(size)])


def iota(rows, columns, axis):
    return lax.broadcasted_iota(jnp.int32, (rows, columns), axis)


def ones_where(condition):
    return jnp.where(condition, 1.0, 0.0).astype(BF16)


def routing(ids_ref, experts):
    tokens = ids_ref.shape[1]
    expert = iota(experts, tokens, 0)
    first = ids_ref[0:1, :] == expert
    second = ids_ref[1:2, :] == expert
    named = ones_where(first | second)
    earlier = ones_where(iota(tokens, tokens, 0) < iota(tokens, tokens, 1))
    ranks = dot(named, earlier, 1, 0)
    return first, second, named, ranks.astype(BF16)


def dispatch_kernel(core_ref, ids_ref, both_ref, send_ref):
    chunk = 2 * SLOTS
    rows = send_ref.shape[0]
    experts, tokens = rows // chunk, ids_ref.shape[1]
    _, _, named, ranks = routing(ids_ref, experts)
    spread = ones_where(iota(rows, experts, 0) // chunk == iota(rows, experts, 1))
    spread_named = dot(spread, named, 1, 0)
    spread_ranks = dot(spread, ranks, 1, 0)
    place = iota(rows, tokens, 0) % chunk
    wanted = (place % SLOTS + SLOTS * core_ref[0]).astype(F32)
    chosen = (spread_named > 0.5) & (spread_ranks == wanted)
    select = jnp.concatenate(
        [ones_where(chosen & (place < SLOTS)), ones_where(chosen & (place >= SLOTS))], axis=1
    )
    send_ref[...] = dot(select, both_ref[...], 1, 1).astype(BF16)


def weight_kernel(core_ref, ids_ref, probs_ref, weight_ref):
    rows = weight_ref.shape[0]
    experts, tokens = rows // SLOTS, ids_ref.shape[1]
    first, second, named, ranks = routing(ids_ref, experts)
    probs = jnp.where(first, probs_ref[0:1, :], 0.0) + jnp.where(second, probs_ref[1:2, :], 0.0)
    high = probs.astype(BF16)
    low = (probs - high.astype(F32)).astype(BF16)
    spread = ones_where(iota(rows, experts, 0) // SLOTS == iota(rows, experts, 1))
    wanted = (iota(rows, tokens, 0) % SLOTS + SLOTS * core_ref[0]).astype(F32)
    chosen = (dot(spread, named, 1, 0) > 0.5) & (dot(spread, ranks, 1, 0) == wanted)
    parts = [jnp.where(chosen, dot(spread, part, 1, 0), 0.0).astype(BF16) for part in (high, low)]
    weight_ref[...] = jnp.concatenate(parts, axis=1)


def call(kernel, shape, arrays, flops):
    whole = pl.BlockSpec(memory_space=pltpu.VMEM)
    return pl.pallas_call(
        kernel,
        out_shape=jax.ShapeDtypeStruct(shape, BF16),
        in_specs=[pl.BlockSpec(memory_space=pltpu.SMEM)] + [whole] * (len(arrays) - 1),
        out_specs=whole,
        compiler_params=pltpu.CompilerParams(vmem_limit_bytes=24 * 1024 * 1024),
        cost_estimate=pl.CostEstimate(flops=flops, bytes_accessed=2 * shape[0] * shape[1], transcendentals=0),
    )(*arrays)


def shards(layer_input, out_grad, expert_ids, gate_probs, w_gate, w_up, w_down):
    groups = N_Z * N_X
    tokens, width = layer_input.shape
    rows = groups * SLOTS
    chip = N_C * width
    core = lax.axis_index("c")
    here = lax.axis_index("y")
    core_ref = core.astype(jnp.int32).reshape(1)

    own = jnp.concatenate([layer_input.T, out_grad.T], axis=1)
    both = lax.all_gather(own, "c", axis=0, tiled=True)
    send = call(
        dispatch_kernel, (2 * rows, chip), (core_ref, expert_ids.T, both), 4 * rows * chip * tokens
    ).reshape(groups, 2 * SLOTS, chip)
    weights = call(weight_kernel, (rows, 2 * tokens), (core_ref, expert_ids.T, gate_probs.T), rows * tokens * 256)

    send, w_gate, w_up, w_down = lax.optimization_barrier((send, w_gate, w_up, w_down))
    recv = lax.all_to_all(send, GROUP, split_axis=0, concat_axis=0, tiled=True).reshape(2 * rows, chip)

    mats = jnp.stack([w_gate[0], w_up[0], w_down[0].T])

    def part(step):
        return lax.dynamic_slice_in_dim(mats, chip * ((here + step) % N_Y), chip, axis=1)

    blocks = [part(0)] + [shift(part(d), "y", d, N_Y) for d in range(1, N_Y)]
    full = [jnp.concatenate([block, shift(block, "c", 1, N_C)], axis=2) for block in blocks]

    source = 2 * SLOTS * (iota(rows, 2 * rows, 0) // SLOTS) + iota(rows, 2 * rows, 0) % SLOTS
    place = iota(rows, 2 * rows, 1)
    rows_in = dot(ones_where(place == source), recv, 1, 0).astype(BF16)
    rows_grad = dot(ones_where(place == source + SLOTS), recv, 1, 0).astype(BF16)

    def partial(d):
        return jnp.stack(
            [dot(rows_in, full[d][0], 1, 0), dot(rows_in, full[d][1], 1, 0), dot(rows_grad, full[d][2], 1, 0)]
        )

    sums = partial(0)
    for d in (2, 1, 3):
        sums = sums + shift(partial(d).astype(BF16), "y", -d, N_Y).astype(F32)
    gate_act, up_act, hidden_grad = sums[0], sums[1], sums[2]
    sigmoid_gate = jax.nn.sigmoid(gate_act)
    gate_grad = hidden_grad * up_act * sigmoid_gate * (1.0 + gate_act * (1.0 - sigmoid_gate))
    up_grad = hidden_grad * gate_act * sigmoid_gate
    grads = jnp.stack([gate_grad.astype(BF16), up_grad.astype(BF16)])
    back = jnp.zeros((rows, chip), F32)
    for d in range(N_Y):
        theirs = shift(grads, "y", d, N_Y) if d else grads
        back = back + dot(theirs[0], full[d][0], 1, 1) + dot(theirs[1], full[d][1], 1, 1)

    returned = lax.all_to_all(
        back.astype(BF16).reshape(groups, SLOTS, chip), GROUP, split_axis=0, concat_axis=0, tiled=True
    ).reshape(rows, chip)
    mixed = dot(returned, weights, 0, 0)
    mixed = (mixed[:, :tokens] + mixed[:, tokens:]).reshape(N_C, width, tokens)
    mine = lax.dynamic_index_in_dim(mixed, core, 0, keepdims=False)
    sibling = lax.dynamic_index_in_dim(mixed, 1 - core, 0, keepdims=False)
    result = mine + shift(sibling, "c", 1, N_C)
    return result.astype(BF16).T


def solution(mesh):
    split = Mesh(mesh.devices.reshape(N_Z, N_X, N_Y, N_C), GROUP + LOCAL)
    placed = (
        P(GROUP, LOCAL),
        P(GROUP, LOCAL),
        P(GROUP, None),
        P(GROUP, None),
        P(GROUP, None, LOCAL),
        P(GROUP, None, LOCAL),
        P(GROUP, LOCAL, None),
    )
    return jax.shard_map(
        shards, mesh=split, in_specs=placed, out_specs=P(GROUP, LOCAL), check_vma=False
    )
```

```python
import jax
import jax.numpy as jnp
from jax import lax
from jax.experimental import pallas as pl
from jax.experimental.pallas import tpu as pltpu
from jax.sharding import Mesh, PartitionSpec as P

N_Z, N_X, N_Y, N_C = 16, 4, 4, 2
GROUP = ("z", "x")
LOCAL = ("y", "c")
SLOTS = 4
BF16 = jnp.bfloat16
F32 = jnp.float32


def dot(left, right, left_dim, right_dim):
    return lax.dot_general(
        left, right, (((left_dim,), (right_dim,)), ((), ())), preferred_element_type=F32
    )


def shift(value, axis, step, size):
    return lax.ppermute(value, axis, [(i, (i + step) % size) for i in range(size)])


def iota(rows, columns, axis):
    return lax.broadcasted_iota(jnp.int32, (rows, columns), axis)


def ones_where(condition):
    return jnp.where(condition, 1.0, 0.0).astype(BF16)


def routing(ids_ref, experts):
    tokens = ids_ref.shape[1]
    expert = iota(experts, tokens, 0)
    first = ids_ref[0:1, :] == expert
    second = ids_ref[1:2, :] == expert
    named = ones_where(first | second)
    earlier = ones_where(iota(tokens, tokens, 0) < iota(tokens, tokens, 1))
    ranks = dot(named, earlier, 1, 0)
    return first, second, named, ranks.astype(BF16)


def dispatch_kernel(core_ref, ids_ref, both_ref, send_ref):
    chunk = 2 * SLOTS
    rows = send_ref.shape[0]
    experts, tokens = rows // chunk, ids_ref.shape[1]
    _, _, named, ranks = routing(ids_ref, experts)
    spread = ones_where(iota(rows, experts, 0) // chunk == iota(rows, experts, 1))
    spread_named = dot(spread, named, 1, 0)
    spread_ranks = dot(spread, ranks, 1, 0)
    place = iota(rows, tokens, 0) % chunk
    wanted = (place % SLOTS + SLOTS * core_ref[0]).astype(F32)
    chosen = (spread_named > 0.5) & (spread_ranks == wanted)
    select = jnp.concatenate(
        [ones_where(chosen & (place < SLOTS)), ones_where(chosen & (place >= SLOTS))], axis=1
    )
    send_ref[...] = dot(select, both_ref[...], 1, 1).astype(BF16)


def weight_kernel(core_ref, ids_ref, probs_ref, weight_ref):
    rows = weight_ref.shape[0]
    experts, tokens = rows // SLOTS, ids_ref.shape[1]
    first, second, named, ranks = routing(ids_ref, experts)
    probs = jnp.where(first, probs_ref[0:1, :], 0.0) + jnp.where(second, probs_ref[1:2, :], 0.0)
    high = probs.astype(BF16)
    low = (probs - high.astype(F32)).astype(BF16)
    spread = ones_where(iota(rows, experts, 0) // SLOTS == iota(rows, experts, 1))
    wanted = (iota(rows, tokens, 0) % SLOTS + SLOTS * core_ref[0]).astype(F32)
    chosen = (dot(spread, named, 1, 0) > 0.5) & (dot(spread, ranks, 1, 0) == wanted)
    parts = [jnp.where(chosen, dot(spread, part, 1, 0), 0.0).astype(BF16) for part in (high, low)]
    weight_ref[...] = jnp.concatenate(parts, axis=1)


def activations(rows_in, rows_grad, own_ref, other_ref, part_ref):
    for m, left in enumerate((rows_in, rows_in, rows_grad)):
        right = jnp.concatenate([own_ref[m], other_ref[m]], axis=1)
        part_ref[m] = dot(left, right, 1, 0).astype(part_ref.dtype)


def first_kernel(recv_ref, own_ref, other_ref, in_ref, grad_ref, part_ref):
    recv = recv_ref[...]
    rows_in = recv[:, :SLOTS, :].reshape(in_ref.shape)
    rows_grad = recv[:, SLOTS:, :].reshape(grad_ref.shape)
    in_ref[...] = rows_in
    grad_ref[...] = rows_grad
    activations(rows_in, rows_grad, own_ref, other_ref, part_ref)


def next_kernel(in_ref, grad_ref, own_ref, other_ref, part_ref):
    activations(in_ref[...], grad_ref[...], own_ref, other_ref, part_ref)


def hidden_kernel(first_ref, *refs):
    *others, grads_ref = refs
    gate_act, up_act, hidden_grad = (
        first_ref[m] + sum(other[m].astype(F32) for other in others) for m in range(3)
    )
    sigmoid_gate = jax.nn.sigmoid(gate_act)
    gate_grad = hidden_grad * up_act * sigmoid_gate * (1.0 + gate_act * (1.0 - sigmoid_gate))
    up_grad = hidden_grad * gate_act * sigmoid_gate
    for y in range(N_Y):
        grads_ref[y, 0] = gate_grad.astype(BF16)
        grads_ref[y, 1] = up_grad.astype(BF16)


def back_kernel(here_ref, grads_ref, *refs):
    weights, out_ref = refs[:-1], refs[-1]
    total = None
    for d in range(N_Y):
        own, other = weights[2 * d], weights[2 * d + 1]
        origin = lax.rem(here_ref[0] + N_Y - d, N_Y)
        for m in range(2):
            right = jnp.concatenate([own[m], other[m]], axis=1)
            term = dot(grads_ref[origin, m], right, 1, 1)
            total = term if total is None else total + term
    out_ref[...] = total.reshape(out_ref.shape).astype(BF16)


def call(kernel, shapes, arrays, flops, kind=BF16):
    def place(array):
        return pltpu.SMEM if array.shape == (1,) else pltpu.VMEM

    size = 0
    for shape in shapes:
        length = 2
        for dim in shape:
            length *= dim
        size += length
    out = pl.pallas_call(
        kernel,
        out_shape=[jax.ShapeDtypeStruct(shape, kind) for shape in shapes],
        in_specs=[pl.BlockSpec(memory_space=place(array)) for array in arrays],
        out_specs=[pl.BlockSpec(memory_space=pltpu.VMEM)] * len(shapes),
        compiler_params=pltpu.CompilerParams(vmem_limit_bytes=24 * 1024 * 1024),
        cost_estimate=pl.CostEstimate(flops=flops, bytes_accessed=size, transcendentals=0),
    )(*arrays)
    return out if len(shapes) > 1 else out[0]


def shards(layer_input, out_grad, expert_ids, gate_probs, w_gate, w_up, w_down):
    groups = N_Z * N_X
    tokens, width = layer_input.shape
    rows = groups * SLOTS
    chip = N_C * width
    core = lax.axis_index("c")
    here = lax.axis_index("y")
    core_ref = core.astype(jnp.int32).reshape(1)

    own = jnp.concatenate([layer_input.T, out_grad.T], axis=1)
    both = lax.all_gather(own, "c", axis=0, tiled=True)
    send = call(
        dispatch_kernel, [(2 * rows, chip)], (core_ref, expert_ids.T, both), 4 * rows * chip * tokens
    ).reshape(groups, 2 * SLOTS, chip)
    weights = call(weight_kernel, [(rows, 2 * tokens)], (core_ref, expert_ids.T, gate_probs.T), rows * tokens * 256)

    send, w_gate, w_up, w_down = lax.optimization_barrier((send, w_gate, w_up, w_down))
    recv = lax.all_to_all(send, GROUP, split_axis=0, concat_axis=0, tiled=True)

    mats = jnp.stack([w_gate[0], w_up[0], w_down[0].T])

    def part(step):
        return lax.dynamic_slice_in_dim(mats, chip * ((here + step) % N_Y), chip, axis=1)

    blocks = [part(0)] + [shift(part(d), "y", d, N_Y) for d in range(1, N_Y)]
    pieces = []
    for block in blocks:
        pieces += [block, shift(block, "c", 1, N_C)]

    here_ref = here.astype(jnp.int32).reshape(1)
    units = N_C * w_gate.shape[2]
    product = 2 * rows * chip * units * N_Y
    shape = (3, rows, units)
    rows_in, rows_grad, part = call(
        first_kernel, [(rows, chip), (rows, chip), shape], [recv] + pieces[4:6], 3 * product // N_Y
    )
    parts = [shift(part, "y", -2, N_Y)]
    for d in (1, 3):
        part = call(next_kernel, [shape], [rows_in, rows_grad] + pieces[2 * d : 2 * d + 2], 3 * product // N_Y)
        parts.append(shift(part, "y", -d, N_Y))
    part = call(next_kernel, [shape], [rows_in, rows_grad] + pieces[:2], 3 * product // N_Y, F32)
    grads = call(hidden_kernel, [(N_Y, 2, rows, units)], [part] + parts, 40 * rows * units)
    grads = lax.all_to_all(grads, "y", split_axis=0, concat_axis=0, tiled=True)
    back = call(back_kernel, [(groups, SLOTS, chip)], [here_ref, grads] + pieces, 2 * product)
    returned = lax.all_to_all(back, GROUP, split_axis=0, concat_axis=0, tiled=True).reshape(rows, chip)
    mixed = dot(returned, weights, 0, 0)
    mixed = (mixed[:, :tokens] + mixed[:, tokens:]).reshape(N_C, width, tokens)
    mine = lax.dynamic_index_in_dim(mixed, core, 0, keepdims=False)
    sibling = lax.dynamic_index_in_dim(mixed, 1 - core, 0, keepdims=False)
    result = mine + shift(sibling, "c", 1, N_C)
    return result.astype(BF16).T


def solution(mesh):
    split = Mesh(mesh.devices.reshape(N_Z, N_X, N_Y, N_C), GROUP + LOCAL)
    placed = (
        P(GROUP, LOCAL),
        P(GROUP, LOCAL),
        P(GROUP, None),
        P(GROUP, None),
        P(GROUP, None, LOCAL),
        P(GROUP, None, LOCAL),
        P(GROUP, LOCAL, None),
    )
    return jax.shard_map(
        shards, mesh=split, in_specs=placed, out_specs=P(GROUP, LOCAL), check_vma=False
    )
```

```python
import jax
import jax.numpy as jnp
from jax import lax
from jax.experimental import pallas as pl
from jax.experimental.pallas import tpu as pltpu
from jax.sharding import Mesh, PartitionSpec as P

N_Z, N_X, N_Y, N_C = 16, 4, 4, 2
GROUP = ("z", "x")
LOCAL = ("y", "c")
SLOTS = 4
BF16 = jnp.bfloat16
F32 = jnp.float32


def dot(left, right, left_dim, right_dim):
    return lax.dot_general(
        left, right, (((left_dim,), (right_dim,)), ((), ())), preferred_element_type=F32
    )


def shift(value, axis, step, size):
    return lax.ppermute(value, axis, [(i, (i + step) % size) for i in range(size)])


def iota(rows, columns, axis):
    return lax.broadcasted_iota(jnp.int32, (rows, columns), axis)


def ones_where(condition):
    return jnp.where(condition, 1.0, 0.0).astype(BF16)


def routing(ids_ref, experts):
    tokens = ids_ref.shape[1]
    expert = iota(experts, tokens, 0)
    first = ids_ref[0:1, :] == expert
    second = ids_ref[1:2, :] == expert
    named = ones_where(first | second)
    earlier = ones_where(iota(tokens, tokens, 0) < iota(tokens, tokens, 1))
    ranks = dot(named, earlier, 1, 0)
    return first, second, named, ranks.astype(BF16)


def dispatch_kernel(core_ref, ids_ref, both_ref, send_ref):
    chunk = 2 * SLOTS
    rows = send_ref.shape[0]
    experts, tokens = rows // chunk, ids_ref.shape[1]
    _, _, named, ranks = routing(ids_ref, experts)
    spread = ones_where(iota(rows, experts, 0) // chunk == iota(rows, experts, 1))
    spread_named = dot(spread, named, 1, 0)
    spread_ranks = dot(spread, ranks, 1, 0)
    place = iota(rows, tokens, 0) % chunk
    wanted = (place % SLOTS + SLOTS * core_ref[0]).astype(F32)
    chosen = (spread_named > 0.5) & (spread_ranks == wanted)
    select = jnp.concatenate(
        [ones_where(chosen & (place < SLOTS)), ones_where(chosen & (place >= SLOTS))], axis=1
    )
    send_ref[...] = dot(select, both_ref[...], 1, 1).astype(BF16)


def weight_kernel(core_ref, ids_ref, probs_ref, weight_ref):
    rows = weight_ref.shape[0]
    experts, tokens = rows // SLOTS, ids_ref.shape[1]
    first, second, named, ranks = routing(ids_ref, experts)
    probs = jnp.where(first, probs_ref[0:1, :], 0.0) + jnp.where(second, probs_ref[1:2, :], 0.0)
    high = probs.astype(BF16)
    low = (probs - high.astype(F32)).astype(BF16)
    spread = ones_where(iota(rows, experts, 0) // SLOTS == iota(rows, experts, 1))
    wanted = (iota(rows, tokens, 0) % SLOTS + SLOTS * core_ref[0]).astype(F32)
    chosen = (dot(spread, named, 1, 0) > 0.5) & (dot(spread, ranks, 1, 0) == wanted)
    parts = [jnp.where(chosen, dot(spread, part, 1, 0), 0.0).astype(BF16) for part in (high, low)]
    weight_ref[...] = jnp.concatenate(parts, axis=1)


def middle_kernel(here_ref, recv_ref, *refs):
    pieces, part_ref = refs[: N_Y * N_C], refs[N_Y * N_C]
    recv_held, held, part_held, recv_sem, sems, part_sems = refs[N_Y * N_C + 1 :]
    recv_copy = pltpu.make_async_copy(recv_ref, recv_held, recv_sem)
    recv_copy.start()
    copies = [pltpu.make_async_copy(piece, held.at[i], sems.at[i]) for i, piece in enumerate(pieces)]
    for copy in copies:
        copy.start()
    recv_copy.wait()
    recv = recv_held[...]
    rows_in = recv[:, :SLOTS, :].reshape(-1, recv.shape[2])
    rows_grad = recv[:, SLOTS:, :].reshape(-1, recv.shape[2])
    outs = []
    for d in range(N_Y):
        for i in range(N_C * d, N_C * (d + 1)):
            copies[i].wait()
        for m, left in enumerate((rows_in, rows_in, rows_grad)):
            right = jnp.concatenate([held[N_C * d + c, m] for c in range(N_C)], axis=1)
            part_held[d, m] = dot(left, right, 1, 0).astype(BF16)
        target = lax.rem(here_ref[0] + N_Y - d, N_Y)
        outs.append(pltpu.make_async_copy(part_held.at[d], part_ref.at[target], part_sems.at[d]))
        outs[-1].start()
    for out in outs:
        out.wait()


def hidden_kernel(parts_ref, grads_ref):
    gate_act, up_act, hidden_grad = (
        sum(parts_ref[y, m].astype(F32) for y in range(N_Y)) for m in range(3)
    )
    sigmoid_gate = jax.nn.sigmoid(gate_act)
    gate_grad = hidden_grad * up_act * sigmoid_gate * (1.0 + gate_act * (1.0 - sigmoid_gate))
    up_grad = hidden_grad * gate_act * sigmoid_gate
    for y in range(N_Y):
        grads_ref[y, 0] = gate_grad.astype(BF16)
        grads_ref[y, 1] = up_grad.astype(BF16)


def back_kernel(here_ref, grads_ref, *refs):
    weights, out_ref = refs[:-1], refs[-1]
    total = None
    for d in range(N_Y):
        own, other = weights[2 * d], weights[2 * d + 1]
        origin = lax.rem(here_ref[0] + N_Y - d, N_Y)
        for m in range(2):
            right = jnp.concatenate([own[m], other[m]], axis=1)
            term = dot(grads_ref[origin, m], right, 1, 1)
            total = term if total is None else total + term
    out_ref[...] = total.reshape(out_ref.shape).astype(BF16)


def call(kernel, shape, arrays, flops):
    def place(array):
        return pltpu.SMEM if array.shape == (1,) else pltpu.VMEM

    size = 2
    for dim in shape:
        size *= dim
    return pl.pallas_call(
        kernel,
        out_shape=jax.ShapeDtypeStruct(shape, BF16),
        in_specs=[pl.BlockSpec(memory_space=place(array)) for array in arrays],
        out_specs=pl.BlockSpec(memory_space=pltpu.VMEM),
        compiler_params=pltpu.CompilerParams(vmem_limit_bytes=24 * 1024 * 1024),
        cost_estimate=pl.CostEstimate(flops=flops, bytes_accessed=size, transcendentals=0),
    )(*arrays)


def call_middle(here_ref, recv, pieces):
    groups, chunk, chip = recv.shape
    mats, _, lanes = pieces[0].shape
    rows, units = groups * chunk // 2, N_C * lanes
    parts = (N_Y, mats, rows, units)
    size = 2 * (recv.size + len(pieces) * pieces[0].size + N_Y * mats * rows * units)
    return pl.pallas_call(
        middle_kernel,
        out_shape=jax.ShapeDtypeStruct(parts, BF16),
        in_specs=[pl.BlockSpec(memory_space=pltpu.SMEM)] + [pl.BlockSpec(memory_space=pl.ANY)] * (1 + len(pieces)),
        out_specs=pl.BlockSpec(memory_space=pl.ANY),
        scratch_shapes=[
            pltpu.VMEM(recv.shape, BF16),
            pltpu.VMEM((len(pieces), mats, chip, lanes), BF16),
            pltpu.VMEM(parts, BF16),
            pltpu.SemaphoreType.DMA,
            pltpu.SemaphoreType.DMA((len(pieces),)),
            pltpu.SemaphoreType.DMA((N_Y,)),
        ],
        compiler_params=pltpu.CompilerParams(vmem_limit_bytes=60 * 1024 * 1024),
        cost_estimate=pl.CostEstimate(
            flops=2 * rows * chip * units * N_Y * mats, bytes_accessed=size, transcendentals=0
        ),
    )(here_ref, recv, *pieces)


def shards(layer_input, out_grad, expert_ids, gate_probs, w_gate, w_up, w_down):
    groups = N_Z * N_X
    tokens, width = layer_input.shape
    rows = groups * SLOTS
    chip = N_C * width
    core = lax.axis_index("c")
    here = lax.axis_index("y")
    core_ref = core.astype(jnp.int32).reshape(1)

    own = jnp.concatenate([layer_input.T, out_grad.T], axis=1)
    both = lax.all_gather(own, "c", axis=0, tiled=True)
    send = call(
        dispatch_kernel, (2 * rows, chip), (core_ref, expert_ids.T, both), 4 * rows * chip * tokens
    ).reshape(groups, 2 * SLOTS, chip)
    weights = call(weight_kernel, (rows, 2 * tokens), (core_ref, expert_ids.T, gate_probs.T), rows * tokens * 256)

    send, w_gate, w_up, w_down = lax.optimization_barrier((send, w_gate, w_up, w_down))
    recv = lax.all_to_all(send, GROUP, split_axis=0, concat_axis=0, tiled=True)

    mats = jnp.stack([w_gate[0], w_up[0], w_down[0].T])

    def part(step):
        return lax.dynamic_slice_in_dim(mats, chip * ((here + step) % N_Y), chip, axis=1)

    blocks = [part(0)] + [shift(part(d), "y", d, N_Y) for d in range(1, N_Y)]
    others = [shift(blocks[0], "c", 1, N_C)]
    others[0], blocks[2] = lax.optimization_barrier((others[0], blocks[2]))
    others += [shift(block, "c", 1, N_C) for block in blocks[1:]]
    pieces = [piece for pair in zip(blocks, others) for piece in pair]

    here_ref = here.astype(jnp.int32).reshape(1)
    units = N_C * w_gate.shape[2]
    product = 2 * rows * chip * units * N_Y
    parts = call_middle(here_ref, recv, pieces)
    parts = lax.all_to_all(parts, "y", split_axis=0, concat_axis=0, tiled=True)
    grads = call(hidden_kernel, (N_Y, 2, rows, units), [parts], 40 * rows * units)
    grads = lax.all_to_all(grads, "y", split_axis=0, concat_axis=0, tiled=True)
    back = call(back_kernel, (groups, SLOTS, chip), [here_ref, grads] + pieces, 2 * product)
    returned = lax.all_to_all(back, GROUP, split_axis=0, concat_axis=0, tiled=True).reshape(rows, chip)
    mixed = dot(returned, weights, 0, 0)
    mixed = (mixed[:, :tokens] + mixed[:, tokens:]).reshape(N_C, width, tokens)
    mine = lax.dynamic_index_in_dim(mixed, core, 0, keepdims=False)
    sibling = lax.dynamic_index_in_dim(mixed, 1 - core, 0, keepdims=False)
    sent = lax.all_gather(sibling, "c", axis=0)
    result = mine + lax.dynamic_index_in_dim(sent, 1 - core, 0, keepdims=False)
    return result.astype(BF16).T


def solution(mesh):
    split = Mesh(mesh.devices.reshape(N_Z, N_X, N_Y, N_C), GROUP + LOCAL)
    placed = (
        P(GROUP, LOCAL),
        P(GROUP, LOCAL),
        P(GROUP, None),
        P(GROUP, None),
        P(GROUP, None, LOCAL),
        P(GROUP, None, LOCAL),
        P(GROUP, LOCAL, None),
    )
    return jax.shard_map(
        shards, mesh=split, in_specs=placed, out_specs=P(GROUP, LOCAL), check_vma=False
    )
```

```python
import jax
import jax.numpy as jnp
from jax import lax
from jax.experimental import pallas as pl
from jax.experimental.pallas import tpu as pltpu
from jax.sharding import Mesh, PartitionSpec as P

N_Z, N_X, N_Y, N_C = 16, 4, 4, 2
GROUP = ("z", "x")
LOCAL = ("y", "c")
SLOTS = 4
BF16 = jnp.bfloat16
F32 = jnp.float32


def dot(left, right, left_dim, right_dim):
    return lax.dot_general(
        left, right, (((left_dim,), (right_dim,)), ((), ())), preferred_element_type=F32
    )


def shift(value, axis, step, size):
    return lax.ppermute(value, axis, [(i, (i + step) % size) for i in range(size)])


def iota(rows, columns, axis):
    return lax.broadcasted_iota(jnp.int32, (rows, columns), axis)


def ones_where(condition):
    return jnp.where(condition, 1.0, 0.0).astype(BF16)


def routing(ids_ref, experts):
    tokens = ids_ref.shape[1]
    expert = iota(experts, tokens, 0)
    first = ids_ref[0:1, :] == expert
    second = ids_ref[1:2, :] == expert
    named = ones_where(first | second)
    earlier = ones_where(iota(tokens, tokens, 0) < iota(tokens, tokens, 1))
    ranks = dot(named, earlier, 1, 0)
    return first, second, named, ranks.astype(BF16)


def select_kernel(core_ref, ids_ref, in_ref, grad_ref, own_ref, select_ref, ids_held, sems):
    tokens = ids_ref.shape[1]
    copies = [
        pltpu.make_async_copy(ids_ref, ids_held, sems.at[0]),
        pltpu.make_async_copy(in_ref, own_ref.at[:, pl.ds(0, tokens)], sems.at[1]),
        pltpu.make_async_copy(grad_ref, own_ref.at[:, pl.ds(tokens, tokens)], sems.at[2]),
    ]
    for copy in copies:
        copy.start()
    chunk = 2 * SLOTS
    rows = select_ref.shape[0]
    experts = rows // chunk
    copies[0].wait()
    _, _, named, ranks = routing(ids_held, experts)
    spread = ones_where(iota(rows, experts, 0) // chunk == iota(rows, experts, 1))
    spread_named = dot(spread, named, 1, 0)
    spread_ranks = dot(spread, ranks, 1, 0)
    place = iota(rows, tokens, 0) % chunk
    wanted = (place % SLOTS + SLOTS * core_ref[0]).astype(F32)
    chosen = (spread_named > 0.5) & (spread_ranks == wanted)
    select_ref[:, :tokens] = ones_where(chosen & (place < SLOTS))
    select_ref[:, tokens:] = ones_where(chosen & (place >= SLOTS))
    copies[1].wait()
    copies[2].wait()


def weight_kernel(core_ref, ids_ref, probs_ref, weight_ref):
    rows = weight_ref.shape[0]
    experts, tokens = rows // SLOTS, ids_ref.shape[1]
    first, second, named, ranks = routing(ids_ref, experts)
    probs = jnp.where(first, probs_ref[0:1, :], 0.0) + jnp.where(second, probs_ref[1:2, :], 0.0)
    high = probs.astype(BF16)
    low = (probs - high.astype(F32)).astype(BF16)
    spread = ones_where(iota(rows, experts, 0) // SLOTS == iota(rows, experts, 1))
    wanted = (iota(rows, tokens, 0) % SLOTS + SLOTS * core_ref[0]).astype(F32)
    chosen = (dot(spread, named, 1, 0) > 0.5) & (dot(spread, ranks, 1, 0) == wanted)
    parts = [jnp.where(chosen, dot(spread, part, 1, 0), 0.0).astype(BF16) for part in (high, low)]
    weight_ref[...] = jnp.concatenate(parts, axis=1)


def units_of(block, other, m):
    return jnp.concatenate([block[m], other[m]], axis=1)


def first_kernel(recv_ref, block_ref, other_ref, in_ref, grad_ref, part_ref):
    recv = recv_ref[...]
    rows_in = recv[:, :SLOTS, :].reshape(in_ref.shape)
    rows_grad = recv[:, SLOTS:, :].reshape(grad_ref.shape)
    in_ref[...] = rows_in
    grad_ref[...] = rows_grad
    for m, left in enumerate((rows_in, rows_in, rows_grad)):
        part_ref[m] = dot(left, units_of(block_ref, other_ref, m), 1, 0).astype(BF16)


def next_kernel(in_ref, grad_ref, block_ref, other_ref, part_ref):
    for m, left in enumerate((in_ref, in_ref, grad_ref)):
        part_ref[m] = dot(left[...], units_of(block_ref, other_ref, m), 1, 0).astype(BF16)


def own_kernel(in_ref, grad_ref, block_ref, other_ref, arrived_ref, part_ref):
    for m, left in enumerate((in_ref, in_ref, grad_ref)):
        part = dot(left[...], units_of(block_ref, other_ref, m), 1, 0)
        part_ref[m] = part + arrived_ref[m].astype(F32)


def hidden_kernel(own_ref, next_ref, last_ref, grads_ref):
    gate_act, up_act, hidden_grad = (
        own_ref[m] + next_ref[m].astype(F32) + last_ref[m].astype(F32) for m in range(3)
    )
    sigmoid_gate = jax.nn.sigmoid(gate_act)
    gate_grad = hidden_grad * up_act * sigmoid_gate * (1.0 + gate_act * (1.0 - sigmoid_gate))
    up_grad = hidden_grad * gate_act * sigmoid_gate
    for y in range(N_Y):
        grads_ref[y, 0] = gate_grad.astype(BF16)
        grads_ref[y, 1] = up_grad.astype(BF16)


def back_kernel(here_ref, grads_ref, *refs):
    blocks, others, out_ref = refs[:N_Y], refs[N_Y:-1], refs[-1]
    total = None
    for d in range(N_Y):
        origin = lax.rem(here_ref[0] + N_Y - d, N_Y)
        for m in range(2):
            term = dot(grads_ref[origin, m], units_of(blocks[d], others[d], m), 1, 1)
            total = term if total is None else total + term
    out_ref[...] = total.reshape(out_ref.shape).astype(BF16)


def call(kernel, shapes, arrays, flops, kind=BF16):
    def place(array):
        return pltpu.SMEM if array.shape == (1,) else pltpu.VMEM

    size = 0
    for shape in shapes:
        length = 2
        for dim in shape:
            length *= dim
        size += length
    out = pl.pallas_call(
        kernel,
        out_shape=[jax.ShapeDtypeStruct(shape, kind) for shape in shapes],
        in_specs=[pl.BlockSpec(memory_space=place(array)) for array in arrays],
        out_specs=[pl.BlockSpec(memory_space=pltpu.VMEM)] * len(shapes),
        compiler_params=pltpu.CompilerParams(vmem_limit_bytes=24 * 1024 * 1024),
        cost_estimate=pl.CostEstimate(flops=flops, bytes_accessed=size, transcendentals=0),
    )(*arrays)
    return out if len(shapes) > 1 else out[0]


def call_select(core_ref, ids, layer_input, out_grad, rows):
    width, tokens = layer_input.shape
    return pl.pallas_call(
        select_kernel,
        out_shape=[
            jax.ShapeDtypeStruct((width, 2 * tokens), BF16),
            jax.ShapeDtypeStruct((rows, 2 * tokens), BF16),
        ],
        in_specs=[pl.BlockSpec(memory_space=pltpu.SMEM)] + [pl.BlockSpec(memory_space=pl.ANY)] * 3,
        out_specs=[pl.BlockSpec(memory_space=pltpu.VMEM)] * 2,
        scratch_shapes=[pltpu.VMEM(ids.shape, jnp.int32), pltpu.SemaphoreType.DMA((3,))],
        compiler_params=pltpu.CompilerParams(vmem_limit_bytes=60 * 1024 * 1024),
        cost_estimate=pl.CostEstimate(
            flops=rows * tokens * 300, bytes_accessed=4 * tokens * (2 * width + rows), transcendentals=0
        ),
    )(core_ref, ids, layer_input, out_grad)


def shards(layer_input, out_grad, expert_ids, gate_probs, w_gate, w_up, w_down):
    groups = N_Z * N_X
    tokens, width = layer_input.shape
    rows = groups * SLOTS
    chip = N_C * width
    core = lax.axis_index("c")
    here = lax.axis_index("y")
    core_ref = core.astype(jnp.int32).reshape(1)

    own, select = call_select(core_ref, expert_ids.T, layer_input.T, out_grad.T, 2 * rows)
    both = lax.all_gather(own, "c", axis=0, tiled=True)
    send = dot(select, both, 1, 1).astype(BF16).reshape(groups, 2 * SLOTS, chip)
    weights = call(weight_kernel, [(rows, 2 * tokens)], (core_ref, expert_ids.T, gate_probs.T), rows * tokens * 256)

    send, w_gate, w_up, w_down = lax.optimization_barrier((send, w_gate, w_up, w_down))
    recv = lax.all_to_all(send, GROUP, split_axis=0, concat_axis=0, tiled=True)

    mats = jnp.stack([w_gate[0], w_up[0], w_down[0].T])

    def part(step):
        return lax.dynamic_slice_in_dim(mats, chip * ((here + step) % N_Y), chip, axis=1)

    blocks = [part(0)] + [shift(part(d), "y", d, N_Y) for d in range(1, N_Y)]
    other_0, other_1, other_2, other_3 = (shift(block, "c", 1, N_C) for block in blocks)

    here_ref = here.astype(jnp.int32).reshape(1)
    units = N_C * w_gate.shape[2]
    shape = (3, rows, units)
    product = 2 * rows * chip * units
    rows_in, rows_grad, part_2 = call(
        first_kernel, [(rows, chip), (rows, chip), shape], [recv, blocks[2], other_2], 3 * product
    )
    arrived = shift(part_2, "y", -2, N_Y)
    part_1 = call(next_kernel, [shape], [rows_in, rows_grad, blocks[1], other_1], 3 * product)
    part_1 = shift(part_1, "y", -1, N_Y)
    part_3 = call(next_kernel, [shape], [rows_in, rows_grad, blocks[3], other_3], 3 * product)
    part_3 = shift(part_3, "y", -3, N_Y)
    part_0 = call(own_kernel, [shape], [rows_in, rows_grad, blocks[0], other_0, arrived], 3 * product, F32)
    grads = call(hidden_kernel, [(N_Y, 2, rows, units)], [part_0, part_1, part_3], 40 * rows * units)
    grads = lax.all_to_all(grads, "y", split_axis=0, concat_axis=0, tiled=True)
    back = call(
        back_kernel, [(groups, SLOTS, chip)], [here_ref, grads, *blocks, other_0, other_1, other_2, other_3], 8 * product
    )
    returned = lax.all_to_all(back, GROUP, split_axis=0, concat_axis=0, tiled=True).reshape(rows, chip)
    mixed = dot(returned, weights, 0, 0)
    mixed = (mixed[:, :tokens] + mixed[:, tokens:]).reshape(N_C, width, tokens)
    mine = lax.dynamic_index_in_dim(mixed, core, 0, keepdims=False)
    sibling = lax.dynamic_index_in_dim(mixed, 1 - core, 0, keepdims=False)
    sent = lax.all_gather(sibling, "c", axis=0)
    result = mine + lax.dynamic_index_in_dim(sent, 1 - core, 0, keepdims=False)
    return result.astype(BF16).T


def solution(mesh):
    split = Mesh(mesh.devices.reshape(N_Z, N_X, N_Y, N_C), GROUP + LOCAL)
    placed = (
        P(GROUP, LOCAL),
        P(GROUP, LOCAL),
        P(GROUP, None),
        P(GROUP, None),
        P(GROUP, None, LOCAL),
        P(GROUP, None, LOCAL),
        P(GROUP, LOCAL, None),
    )
    return jax.shard_map(
        shards, mesh=split, in_specs=placed, out_specs=P(GROUP, LOCAL), check_vma=False
    )
```

```python
import jax
import jax.numpy as jnp
from jax import lax
from jax.experimental import pallas as pl
from jax.experimental.pallas import tpu as pltpu
from jax.sharding import Mesh, PartitionSpec as P

N_Z, N_X, N_Y, N_C = 16, 4, 4, 2
GROUP = ("z", "x")
LOCAL = ("y", "c")
SLOTS = 4
PAD = 16
BF16 = jnp.bfloat16
F32 = jnp.float32


def dot(left, right, left_dim, right_dim):
    return lax.dot_general(
        left, right, (((left_dim,), (right_dim,)), ((), ())), preferred_element_type=F32
    )


def shift(value, axis, step, size):
    return lax.ppermute(value, axis, [(i, (i + step) % size) for i in range(size)])


def iota(rows, columns, axis):
    return lax.broadcasted_iota(jnp.int32, (rows, columns), axis)


def ones_where(condition):
    return jnp.where(condition, 1.0, 0.0).astype(BF16)


def routing(ids, experts):
    tokens = ids.shape[1]
    expert = iota(experts, tokens, 0).astype(ids.dtype)
    first = ids[0:1, :] == expert
    second = ids[1:2, :] == expert
    named = ones_where(first | second)
    earlier = ones_where(iota(tokens, tokens, 0) < iota(tokens, tokens, 1))
    ranks = dot(named, earlier, 1, 0)
    return first, second, named, ranks.astype(BF16)


def pack_kernel(ids_ref, in_ref, grad_ref, own_ref, ids_held, sems):
    width, tokens = in_ref.shape
    copies = [
        pltpu.make_async_copy(ids_ref, ids_held, sems.at[0]),
        pltpu.make_async_copy(in_ref, own_ref.at[pl.ds(0, width), pl.ds(0, tokens)], sems.at[1]),
        pltpu.make_async_copy(grad_ref, own_ref.at[pl.ds(0, width), pl.ds(tokens, tokens)], sems.at[2]),
    ]
    for copy in copies:
        copy.start()
    copies[0].wait()
    ids = ids_held[...].astype(F32)
    row = iota(PAD, tokens, 0)
    under = jnp.where(row == 0, ids[0:1, :], jnp.where(row == 1, ids[1:2, :], 0.0)).astype(BF16)
    own_ref[width : width + PAD, :tokens] = under
    own_ref[width : width + PAD, tokens:] = jnp.zeros_like(under)
    copies[1].wait()
    copies[2].wait()


def dispatch_kernel(core_ref, both_ref, send_ref):
    groups, chunk, chip = send_ref.shape
    rows, width, tokens = groups * chunk, chip // N_C, both_ref.shape[1] // 2
    _, _, named, ranks = routing(both_ref[width : width + PAD, :tokens].astype(F32), groups)
    spread = ones_where(iota(rows, groups, 0) // chunk == iota(rows, groups, 1))
    spread_named = dot(spread, named, 1, 0)
    spread_ranks = dot(spread, ranks, 1, 0)
    place = iota(rows, tokens, 0) % chunk
    wanted = (place % SLOTS + SLOTS * core_ref[0]).astype(F32)
    chosen = (spread_named > 0.5) & (spread_ranks == wanted)
    select = jnp.concatenate(
        [ones_where(chosen & (place < SLOTS)), ones_where(chosen & (place >= SLOTS))], axis=1
    )
    both = jnp.concatenate([both_ref[c * (width + PAD) : c * (width + PAD) + width] for c in range(N_C)], axis=0)
    send_ref[...] = dot(select, both, 1, 1).reshape(send_ref.shape).astype(BF16)


def weight_kernel(core_ref, ids_ref, probs_ref, weight_ref):
    rows = weight_ref.shape[0]
    experts, tokens = rows // SLOTS, ids_ref.shape[1]
    first, second, named, ranks = routing(ids_ref[...], experts)
    probs = jnp.where(first, probs_ref[0:1, :], 0.0) + jnp.where(second, probs_ref[1:2, :], 0.0)
    high = probs.astype(BF16)
    low = (probs - high.astype(F32)).astype(BF16)
    spread = ones_where(iota(rows, experts, 0) // SLOTS == iota(rows, experts, 1))
    wanted = (iota(rows, tokens, 0) % SLOTS + SLOTS * core_ref[0]).astype(F32)
    chosen = (dot(spread, named, 1, 0) > 0.5) & (dot(spread, ranks, 1, 0) == wanted)
    parts = [jnp.where(chosen, dot(spread, part, 1, 0), 0.0).astype(BF16) for part in (high, low)]
    weight_ref[...] = jnp.concatenate(parts, axis=1)


def units_of(block, other, m):
    return jnp.concatenate([block[m], other[m]], axis=1)


def first_kernel(recv_ref, block_ref, other_ref, in_ref, grad_ref, part_ref):
    recv = recv_ref[...]
    rows_in = recv[:, :SLOTS, :].reshape(in_ref.shape)
    rows_grad = recv[:, SLOTS:, :].reshape(grad_ref.shape)
    in_ref[...] = rows_in
    grad_ref[...] = rows_grad
    for m, left in enumerate((rows_in, rows_in, rows_grad)):
        part_ref[m] = dot(left, units_of(block_ref, other_ref, m), 1, 0).astype(BF16)


def next_kernel(in_ref, grad_ref, block_ref, other_ref, part_ref):
    for m, left in enumerate((in_ref, in_ref, grad_ref)):
        part_ref[m] = dot(left[...], units_of(block_ref, other_ref, m), 1, 0).astype(BF16)


def own_kernel(in_ref, grad_ref, block_ref, other_ref, arrived_ref, part_ref):
    for m, left in enumerate((in_ref, in_ref, grad_ref)):
        part = dot(left[...], units_of(block_ref, other_ref, m), 1, 0)
        part_ref[m] = part + arrived_ref[m].astype(F32)


def hidden_kernel(own_ref, next_ref, last_ref, grads_ref):
    gate_act, up_act, hidden_grad = (
        own_ref[m] + next_ref[m].astype(F32) + last_ref[m].astype(F32) for m in range(3)
    )
    sigmoid_gate = jax.nn.sigmoid(gate_act)
    gate_grad = hidden_grad * up_act * sigmoid_gate * (1.0 + gate_act * (1.0 - sigmoid_gate))
    up_grad = hidden_grad * gate_act * sigmoid_gate
    for y in range(N_Y):
        grads_ref[y, 0] = gate_grad.astype(BF16)
        grads_ref[y, 1] = up_grad.astype(BF16)


def back_kernel(here_ref, grads_ref, *refs):
    blocks, others, out_ref = refs[:N_Y], refs[N_Y:-1], refs[-1]
    origins = [lax.rem(here_ref[0] + N_Y - d, N_Y) for d in range(N_Y)]
    left = jnp.concatenate([grads_ref[origins[d], m] for d in range(N_Y) for m in range(2)], axis=1)
    right = jnp.concatenate([units_of(blocks[d], others[d], m) for d in range(N_Y) for m in range(2)], axis=1)
    total = dot(left, right, 1, 1)
    out_ref[...] = total.reshape(out_ref.shape).astype(BF16)


def call(kernel, shapes, arrays, flops, kind=BF16):
    def place(array):
        return pltpu.SMEM if array.shape == (1,) else pltpu.VMEM

    size = 0
    for shape in shapes:
        length = 2
        for dim in shape:
            length *= dim
        size += length
    out = pl.pallas_call(
        kernel,
        out_shape=[jax.ShapeDtypeStruct(shape, kind) for shape in shapes],
        in_specs=[pl.BlockSpec(memory_space=place(array)) for array in arrays],
        out_specs=[pl.BlockSpec(memory_space=pltpu.VMEM)] * len(shapes),
        compiler_params=pltpu.CompilerParams(vmem_limit_bytes=24 * 1024 * 1024),
        cost_estimate=pl.CostEstimate(flops=flops, bytes_accessed=size, transcendentals=0),
    )(*arrays)
    return out if len(shapes) > 1 else out[0]


def call_pack(ids, layer_input, out_grad):
    width, tokens = layer_input.shape
    return pl.pallas_call(
        pack_kernel,
        out_shape=jax.ShapeDtypeStruct((width + PAD, 2 * tokens), BF16),
        in_specs=[pl.BlockSpec(memory_space=pl.ANY)] * 3,
        out_specs=pl.BlockSpec(memory_space=pltpu.VMEM),
        scratch_shapes=[pltpu.VMEM(ids.shape, jnp.int32), pltpu.SemaphoreType.DMA((3,))],
        compiler_params=pltpu.CompilerParams(vmem_limit_bytes=60 * 1024 * 1024),
        cost_estimate=pl.CostEstimate(flops=0, bytes_accessed=8 * tokens * width, transcendentals=0),
    )(ids, layer_input, out_grad)


def shards(layer_input, out_grad, expert_ids, gate_probs, w_gate, w_up, w_down):
    groups = N_Z * N_X
    tokens, width = layer_input.shape
    rows = groups * SLOTS
    chip = N_C * width
    core = lax.axis_index("c")
    here = lax.axis_index("y")
    core_ref = core.astype(jnp.int32).reshape(1)

    both = lax.all_gather(call_pack(expert_ids.T, layer_input.T, out_grad.T), "c", axis=0, tiled=True)
    send = call(dispatch_kernel, [(groups, 2 * SLOTS, chip)], [core_ref, both], 8 * rows * chip * tokens)
    weights = call(weight_kernel, [(rows, 2 * tokens)], (core_ref, expert_ids.T, gate_probs.T), rows * tokens * 256)

    send, w_gate, w_up, w_down = lax.optimization_barrier((send, w_gate, w_up, w_down))
    recv = lax.all_to_all(send, GROUP, split_axis=0, concat_axis=0, tiled=True)

    mats = jnp.stack([w_gate[0], w_up[0], w_down[0].T])

    def part(step):
        return lax.dynamic_slice_in_dim(mats, chip * ((here + step) % N_Y), chip, axis=1)

    blocks = [part(0)] + [shift(part(d), "y", d, N_Y) for d in range(1, N_Y)]
    other_0, other_1, other_2, other_3 = (shift(block, "c", 1, N_C) for block in blocks)

    here_ref = here.astype(jnp.int32).reshape(1)
    units = N_C * w_gate.shape[2]
    shape = (3, rows, units)
    product = 2 * rows * chip * units
    rows_in, rows_grad, part_2 = call(
        first_kernel, [(rows, chip), (rows, chip), shape], [recv, blocks[2], other_2], 3 * product
    )
    arrived = shift(part_2, "y", -2, N_Y)
    part_1 = call(next_kernel, [shape], [rows_in, rows_grad, blocks[1], other_1], 3 * product)
    part_1 = shift(part_1, "y", -1, N_Y)
    part_3 = call(next_kernel, [shape], [rows_in, rows_grad, blocks[3], other_3], 3 * product)
    part_3 = shift(part_3, "y", -3, N_Y)
    part_0 = call(own_kernel, [shape], [rows_in, rows_grad, blocks[0], other_0, arrived], 3 * product, F32)
    grads = call(hidden_kernel, [(N_Y, 2, rows, units)], [part_0, part_1, part_3], 40 * rows * units)
    grads = lax.all_to_all(grads, "y", split_axis=0, concat_axis=0, tiled=True)
    back = call(
        back_kernel, [(groups, SLOTS, chip)], [here_ref, grads, *blocks, other_0, other_1, other_2, other_3], 8 * product
    )
    returned = lax.all_to_all(back, GROUP, split_axis=0, concat_axis=0, tiled=True).reshape(rows, chip)
    mixed = dot(returned, weights, 0, 0)
    mixed = (mixed[:, :tokens] + mixed[:, tokens:]).reshape(N_C, width, tokens)
    mine = lax.dynamic_index_in_dim(mixed, core, 0, keepdims=False)
    sibling = lax.dynamic_index_in_dim(mixed, 1 - core, 0, keepdims=False)
    sent = lax.all_gather(sibling, "c", axis=0)
    result = mine + lax.dynamic_index_in_dim(sent, 1 - core, 0, keepdims=False)
    return result.astype(BF16).T


def solution(mesh):
    split = Mesh(mesh.devices.reshape(N_Z, N_X, N_Y, N_C), GROUP + LOCAL)
    placed = (
        P(GROUP, LOCAL),
        P(GROUP, LOCAL),
        P(GROUP, None),
        P(GROUP, None),
        P(GROUP, None, LOCAL),
        P(GROUP, None, LOCAL),
        P(GROUP, LOCAL, None),
    )
    return jax.shard_map(
        shards, mesh=split, in_specs=placed, out_specs=P(GROUP, LOCAL), check_vma=False
    )
```

```python
import jax
import jax.numpy as jnp
from jax import lax
from jax.experimental import pallas as pl
from jax.experimental.pallas import tpu as pltpu
from jax.sharding import Mesh, PartitionSpec as P

N_Z, N_X, N_Y, N_C = 16, 4, 4, 2
GROUP = ("z", "x")
LOCAL = ("y", "c")
ORDER = ("x", "z")
SLOTS = 4
PAD = 16
BF16 = jnp.bfloat16
F32 = jnp.float32


def dot(left, right, left_dim, right_dim):
    return lax.dot_general(
        left, right, (((left_dim,), (right_dim,)), ((), ())), preferred_element_type=F32
    )


def shift(value, axis, step, size):
    return lax.ppermute(value, axis, [(i, (i + step) % size) for i in range(size)])


def iota(rows, columns, axis):
    return lax.broadcasted_iota(jnp.int32, (rows, columns), axis)


def ones_where(condition):
    return jnp.where(condition, 1.0, 0.0).astype(BF16)


def routing(ids, experts):
    tokens = ids.shape[1]
    place = iota(experts, tokens, 0)
    expert = (place % N_Z * N_X + place // N_Z).astype(ids.dtype)
    first = ids[0:1, :] == expert
    second = ids[1:2, :] == expert
    named = ones_where(first | second)
    earlier = ones_where(iota(tokens, tokens, 0) < iota(tokens, tokens, 1))
    ranks = dot(named, earlier, 1, 0)
    return first, second, named, ranks.astype(BF16)


def pack_kernel(ids_ref, in_ref, grad_ref, own_ref, ids_held, sems):
    width, tokens = in_ref.shape
    copies = [
        pltpu.make_async_copy(ids_ref, ids_held, sems.at[0]),
        pltpu.make_async_copy(in_ref, own_ref.at[pl.ds(0, width), pl.ds(0, tokens)], sems.at[1]),
        pltpu.make_async_copy(grad_ref, own_ref.at[pl.ds(0, width), pl.ds(tokens, tokens)], sems.at[2]),
    ]
    for copy in copies:
        copy.start()
    copies[0].wait()
    ids = ids_held[...].astype(F32)
    row = iota(PAD, tokens, 0)
    under = jnp.where(row == 0, ids[0:1, :], jnp.where(row == 1, ids[1:2, :], 0.0)).astype(BF16)
    own_ref[width : width + PAD, :tokens] = under
    own_ref[width : width + PAD, tokens:] = jnp.zeros_like(under)
    copies[1].wait()
    copies[2].wait()


def dispatch_kernel(core_ref, both_ref, send_ref):
    groups, chunk, chip = send_ref.shape
    rows, width, tokens = groups * chunk, chip // N_C, both_ref.shape[1] // 2
    _, _, named, ranks = routing(both_ref[width : width + PAD, :tokens].astype(F32), groups)
    spread = ones_where(iota(rows, groups, 0) // chunk == iota(rows, groups, 1))
    spread_named = dot(spread, named, 1, 0)
    spread_ranks = dot(spread, ranks, 1, 0)
    place = iota(rows, tokens, 0) % chunk
    wanted = (place % SLOTS + SLOTS * core_ref[0]).astype(F32)
    chosen = (spread_named > 0.5) & (spread_ranks == wanted)
    select = jnp.concatenate(
        [ones_where(chosen & (place < SLOTS)), ones_where(chosen & (place >= SLOTS))], axis=1
    )
    both = jnp.concatenate([both_ref[c * (width + PAD) : c * (width + PAD) + width] for c in range(N_C)], axis=0)
    send_ref[...] = dot(select, both, 1, 1).reshape(send_ref.shape).astype(BF16)


def weight_kernel(core_ref, ids_ref, probs_ref, weight_ref):
    rows = weight_ref.shape[0]
    experts, tokens = rows // SLOTS, ids_ref.shape[1]
    first, second, named, ranks = routing(ids_ref[...], experts)
    probs = jnp.where(first, probs_ref[0:1, :], 0.0) + jnp.where(second, probs_ref[1:2, :], 0.0)
    high = probs.astype(BF16)
    low = (probs - high.astype(F32)).astype(BF16)
    spread = ones_where(iota(rows, experts, 0) // SLOTS == iota(rows, experts, 1))
    wanted = (iota(rows, tokens, 0) % SLOTS + SLOTS * core_ref[0]).astype(F32)
    chosen = (dot(spread, named, 1, 0) > 0.5) & (dot(spread, ranks, 1, 0) == wanted)
    parts = [jnp.where(chosen, dot(spread, part, 1, 0), 0.0).astype(BF16) for part in (high, low)]
    weight_ref[...] = jnp.concatenate(parts, axis=1)


def units_of(block, other, m):
    return jnp.concatenate([block[m], other[m]], axis=1)


def first_kernel(recv_ref, block_ref, other_ref, in_ref, grad_ref, part_ref):
    recv = recv_ref[...]
    rows_in = recv[:, :SLOTS, :].reshape(in_ref.shape)
    rows_grad = recv[:, SLOTS:, :].reshape(grad_ref.shape)
    in_ref[...] = rows_in
    grad_ref[...] = rows_grad
    for m, left in enumerate((rows_in, rows_in, rows_grad)):
        part_ref[m] = dot(left, units_of(block_ref, other_ref, m), 1, 0).astype(BF16)


def next_kernel(in_ref, grad_ref, block_ref, other_ref, part_ref):
    for m, left in enumerate((in_ref, in_ref, grad_ref)):
        part_ref[m] = dot(left[...], units_of(block_ref, other_ref, m), 1, 0).astype(BF16)


def own_kernel(in_ref, grad_ref, block_ref, other_ref, arrived_ref, part_ref):
    for m, left in enumerate((in_ref, in_ref, grad_ref)):
        part = dot(left[...], units_of(block_ref, other_ref, m), 1, 0)
        part_ref[m] = part + arrived_ref[m].astype(F32)


def hidden_kernel(own_ref, next_ref, last_ref, grads_ref):
    gate_act, up_act, hidden_grad = (
        own_ref[m] + next_ref[m].astype(F32) + last_ref[m].astype(F32) for m in range(3)
    )
    sigmoid_gate = jax.nn.sigmoid(gate_act)
    gate_grad = hidden_grad * up_act * sigmoid_gate * (1.0 + gate_act * (1.0 - sigmoid_gate))
    up_grad = hidden_grad * gate_act * sigmoid_gate
    for y in range(N_Y):
        grads_ref[y, 0] = gate_grad.astype(BF16)
        grads_ref[y, 1] = up_grad.astype(BF16)


def back_kernel(here_ref, grads_ref, *refs):
    blocks, others, out_ref = refs[:N_Y], refs[N_Y:-1], refs[-1]
    origins = [lax.rem(here_ref[0] + N_Y - d, N_Y) for d in range(N_Y)]
    left = jnp.concatenate([grads_ref[origins[d], m] for d in range(N_Y) for m in range(2)], axis=1)
    right = jnp.concatenate([units_of(blocks[d], others[d], m) for d in range(N_Y) for m in range(2)], axis=1)
    total = dot(left, right, 1, 1)
    out_ref[...] = total.reshape(out_ref.shape).astype(BF16)


def call(kernel, shapes, arrays, flops, kind=BF16):
    def place(array):
        return pltpu.SMEM if array.shape == (1,) else pltpu.VMEM

    size = 0
    for shape in shapes:
        length = 2
        for dim in shape:
            length *= dim
        size += length
    out = pl.pallas_call(
        kernel,
        out_shape=[jax.ShapeDtypeStruct(shape, kind) for shape in shapes],
        in_specs=[pl.BlockSpec(memory_space=place(array)) for array in arrays],
        out_specs=[pl.BlockSpec(memory_space=pltpu.VMEM)] * len(shapes),
        compiler_params=pltpu.CompilerParams(vmem_limit_bytes=24 * 1024 * 1024),
        cost_estimate=pl.CostEstimate(flops=flops, bytes_accessed=size, transcendentals=0),
    )(*arrays)
    return out if len(shapes) > 1 else out[0]


def call_pack(ids, layer_input, out_grad):
    width, tokens = layer_input.shape
    return pl.pallas_call(
        pack_kernel,
        out_shape=jax.ShapeDtypeStruct((width + PAD, 2 * tokens), BF16),
        in_specs=[pl.BlockSpec(memory_space=pl.ANY)] * 3,
        out_specs=pl.BlockSpec(memory_space=pltpu.VMEM),
        scratch_shapes=[pltpu.VMEM(ids.shape, jnp.int32), pltpu.SemaphoreType.DMA((3,))],
        compiler_params=pltpu.CompilerParams(vmem_limit_bytes=60 * 1024 * 1024),
        cost_estimate=pl.CostEstimate(flops=0, bytes_accessed=8 * tokens * width, transcendentals=0),
    )(ids, layer_input, out_grad)


def shards(layer_input, out_grad, expert_ids, gate_probs, w_gate, w_up, w_down):
    groups = N_Z * N_X
    tokens, width = layer_input.shape
    rows = groups * SLOTS
    chip = N_C * width
    core = lax.axis_index("c")
    here = lax.axis_index("y")
    core_ref = core.astype(jnp.int32).reshape(1)

    both = lax.all_gather(call_pack(expert_ids.T, layer_input.T, out_grad.T), "c", axis=0, tiled=True)
    send = call(dispatch_kernel, [(groups, 2 * SLOTS, chip)], [core_ref, both], 8 * rows * chip * tokens)
    weights = call(weight_kernel, [(rows, 2 * tokens)], (core_ref, expert_ids.T, gate_probs.T), rows * tokens * 256)

    send, w_gate, w_up, w_down = lax.optimization_barrier((send, w_gate, w_up, w_down))
    recv = lax.all_to_all(send, ORDER, split_axis=0, concat_axis=0, tiled=True)

    mats = jnp.stack([w_gate[0], w_up[0], w_down[0].T])

    def part(step):
        return lax.dynamic_slice_in_dim(mats, chip * ((here + step) % N_Y), chip, axis=1)

    blocks = [part(0)] + [shift(part(d), "y", d, N_Y) for d in range(1, N_Y)]
    other_0, other_1, other_2, other_3 = (shift(block, "c", 1, N_C) for block in blocks)

    here_ref = here.astype(jnp.int32).reshape(1)
    units = N_C * w_gate.shape[2]
    shape = (3, rows, units)
    product = 2 * rows * chip * units
    rows_in, rows_grad, part_2 = call(
        first_kernel, [(rows, chip), (rows, chip), shape], [recv, blocks[2], other_2], 3 * product
    )
    arrived = shift(part_2, "y", -2, N_Y)
    part_1 = call(next_kernel, [shape], [rows_in, rows_grad, blocks[1], other_1], 3 * product)
    part_1 = shift(part_1, "y", -1, N_Y)
    part_3 = call(next_kernel, [shape], [rows_in, rows_grad, blocks[3], other_3], 3 * product)
    part_3 = shift(part_3, "y", -3, N_Y)
    part_0 = call(own_kernel, [shape], [rows_in, rows_grad, blocks[0], other_0, arrived], 3 * product, F32)
    grads = call(hidden_kernel, [(N_Y, 2, rows, units)], [part_0, part_1, part_3], 40 * rows * units)
    grads = lax.all_to_all(grads, "y", split_axis=0, concat_axis=0, tiled=True)
    back = call(
        back_kernel, [(groups, SLOTS, chip)], [here_ref, grads, *blocks, other_0, other_1, other_2, other_3], 8 * product
    )
    returned = lax.all_to_all(back, ORDER, split_axis=0, concat_axis=0, tiled=True).reshape(rows, chip)
    mixed = dot(returned, weights, 0, 0)
    mixed = (mixed[:, :tokens] + mixed[:, tokens:]).reshape(N_C, width, tokens)
    mine = lax.dynamic_index_in_dim(mixed, core, 0, keepdims=False)
    sibling = lax.dynamic_index_in_dim(mixed, 1 - core, 0, keepdims=False)
    sent = lax.all_gather(sibling, "c", axis=0)
    result = mine + lax.dynamic_index_in_dim(sent, 1 - core, 0, keepdims=False)
    return result.astype(BF16).T


def solution(mesh):
    split = Mesh(mesh.devices.reshape(N_Z, N_X, N_Y, N_C), GROUP + LOCAL)
    placed = (
        P(GROUP, LOCAL),
        P(GROUP, LOCAL),
        P(GROUP, None),
        P(GROUP, None),
        P(GROUP, None, LOCAL),
        P(GROUP, None, LOCAL),
        P(GROUP, LOCAL, None),
    )
    return jax.shard_map(
        shards, mesh=split, in_specs=placed, out_specs=P(GROUP, LOCAL), check_vma=False
    )
```

```python
import jax
import jax.numpy as jnp
from jax import lax
from jax.experimental import pallas as pl
from jax.experimental.pallas import tpu as pltpu
from jax.sharding import Mesh, PartitionSpec as P

N_Z, N_X, N_Y, N_C = 16, 4, 4, 2
GROUP = ("z", "x")
LOCAL = ("y", "c")
ORDER = ("x", "z")
SLOTS = 4
PAD = 16
BF16 = jnp.bfloat16
F32 = jnp.float32


def dot(left, right, left_dim, right_dim):
    return lax.dot_general(
        left, right, (((left_dim,), (right_dim,)), ((), ())), preferred_element_type=F32
    )


def shift(value, axis, step, size):
    return lax.ppermute(value, axis, [(i, (i + step) % size) for i in range(size)])


def iota(rows, columns, axis):
    return lax.broadcasted_iota(jnp.int32, (rows, columns), axis)


def ones_where(condition):
    return jnp.where(condition, 1.0, 0.0).astype(BF16)


def routing(ids, experts):
    tokens = ids.shape[1]
    place = iota(experts, tokens, 0)
    expert = (place % N_Z * N_X + place // N_Z).astype(ids.dtype)
    first = ids[0:1, :] == expert
    second = ids[1:2, :] == expert
    named = ones_where(first | second)
    earlier = ones_where(iota(tokens, tokens, 0) < iota(tokens, tokens, 1))
    ranks = dot(named, earlier, 1, 0)
    return first, second, named, ranks.astype(BF16)


def pack_kernel(ids_ref, in_ref, grad_ref, own_ref, ids_held, sems):
    width, tokens = in_ref.shape
    copies = [
        pltpu.make_async_copy(ids_ref, ids_held, sems.at[0]),
        pltpu.make_async_copy(in_ref, own_ref.at[pl.ds(0, width), pl.ds(0, tokens)], sems.at[1]),
        pltpu.make_async_copy(grad_ref, own_ref.at[pl.ds(0, width), pl.ds(tokens, tokens)], sems.at[2]),
    ]
    for copy in copies:
        copy.start()
    copies[0].wait()
    ids = ids_held[...].astype(F32)
    row = iota(PAD, tokens, 0)
    under = jnp.where(row == 0, ids[0:1, :], jnp.where(row == 1, ids[1:2, :], 0.0)).astype(BF16)
    own_ref[width : width + PAD, :tokens] = under
    own_ref[width : width + PAD, tokens:] = jnp.zeros_like(under)
    copies[1].wait()
    copies[2].wait()


def dispatch_kernel(core_ref, both_ref, send_ref):
    groups, chunk, chip = send_ref.shape
    rows, width, tokens = groups * chunk, chip // N_C, both_ref.shape[1] // 2
    _, _, named, ranks = routing(both_ref[width : width + PAD, :tokens].astype(F32), groups)
    spread = ones_where(iota(rows, groups, 0) // chunk == iota(rows, groups, 1))
    spread_named = dot(spread, named, 1, 0)
    spread_ranks = dot(spread, ranks, 1, 0)
    place = iota(rows, tokens, 0) % chunk
    wanted = (place % SLOTS + SLOTS * core_ref[0]).astype(F32)
    chosen = (spread_named > 0.5) & (spread_ranks == wanted)
    select = jnp.concatenate(
        [ones_where(chosen & (place < SLOTS)), ones_where(chosen & (place >= SLOTS))], axis=1
    )
    both = jnp.concatenate([both_ref[c * (width + PAD) : c * (width + PAD) + width] for c in range(N_C)], axis=0)
    send_ref[...] = dot(select, both, 1, 1).reshape(send_ref.shape).astype(BF16)


def weight_kernel(core_ref, ids_ref, probs_ref, weight_ref):
    rows = weight_ref.shape[0]
    experts, tokens = rows // SLOTS, ids_ref.shape[1]
    first, second, named, ranks = routing(ids_ref[...], experts)
    probs = jnp.where(first, probs_ref[0:1, :], 0.0) + jnp.where(second, probs_ref[1:2, :], 0.0)
    high = probs.astype(BF16)
    low = (probs - high.astype(F32)).astype(BF16)
    spread = ones_where(iota(rows, experts, 0) // SLOTS == iota(rows, experts, 1))
    wanted = (iota(rows, tokens, 0) % SLOTS + SLOTS * core_ref[0]).astype(F32)
    chosen = (dot(spread, named, 1, 0) > 0.5) & (dot(spread, ranks, 1, 0) == wanted)
    parts = [jnp.where(chosen, dot(spread, part, 1, 0), 0.0).astype(BF16) for part in (high, low)]
    weight_ref[...] = jnp.concatenate(parts, axis=1)


def units_of(block, other, m):
    return jnp.concatenate([block[m], other[m]], axis=1)


def first_kernel(recv_ref, block_ref, other_ref, in_ref, grad_ref, part_ref):
    recv = recv_ref[...]
    rows_in = recv[:, :SLOTS, :].reshape(in_ref.shape)
    rows_grad = recv[:, SLOTS:, :].reshape(grad_ref.shape)
    in_ref[...] = rows_in
    grad_ref[...] = rows_grad
    for m, left in enumerate((rows_in, rows_in, rows_grad)):
        part_ref[m] = dot(left, units_of(block_ref, other_ref, m), 1, 0).astype(BF16)


def next_kernel(in_ref, grad_ref, block_ref, other_ref, part_ref):
    for m, left in enumerate((in_ref, in_ref, grad_ref)):
        part_ref[m] = dot(left[...], units_of(block_ref, other_ref, m), 1, 0).astype(BF16)


def own_kernel(in_ref, grad_ref, block_ref, other_ref, arrived_ref, part_ref):
    for m, left in enumerate((in_ref, in_ref, grad_ref)):
        part = dot(left[...], units_of(block_ref, other_ref, m), 1, 0)
        part_ref[m] = part + arrived_ref[m].astype(F32)


def hidden_kernel(own_ref, next_ref, last_ref, grads_ref):
    gate_act, up_act, hidden_grad = (
        own_ref[m] + next_ref[m].astype(F32) + last_ref[m].astype(F32) for m in range(3)
    )
    sigmoid_gate = jax.nn.sigmoid(gate_act)
    gate_grad = hidden_grad * up_act * sigmoid_gate * (1.0 + gate_act * (1.0 - sigmoid_gate))
    up_grad = hidden_grad * gate_act * sigmoid_gate
    grads_ref[0] = gate_grad.astype(BF16)
    grads_ref[1] = up_grad.astype(BF16)


def product_back(grads, blocks, others):
    left = jnp.concatenate([grad[m] for grad in grads for m in range(2)], axis=1)
    right = jnp.concatenate([units_of(b, o, m) for b, o in zip(blocks, others) for m in range(2)], axis=1)
    return dot(left, right, 1, 1)


def early_kernel(own_ref, arrived_ref, block_ref, far_ref, other_ref, far_other_ref, total_ref):
    total_ref[...] = product_back((own_ref, arrived_ref), (block_ref, far_ref), (other_ref, far_other_ref))


def back_kernel(total_ref, *refs):
    grads, blocks, others, out_ref = refs[:2], refs[2:4], refs[4:6], refs[6]
    total = total_ref[...] + product_back(grads, blocks, others)
    out_ref[...] = total.reshape(out_ref.shape).astype(BF16)


def call(kernel, shapes, arrays, flops, kind=BF16):
    def place(array):
        return pltpu.SMEM if array.shape == (1,) else pltpu.VMEM

    size = 0
    for shape in shapes:
        length = 2
        for dim in shape:
            length *= dim
        size += length
    out = pl.pallas_call(
        kernel,
        out_shape=[jax.ShapeDtypeStruct(shape, kind) for shape in shapes],
        in_specs=[pl.BlockSpec(memory_space=place(array)) for array in arrays],
        out_specs=[pl.BlockSpec(memory_space=pltpu.VMEM)] * len(shapes),
        compiler_params=pltpu.CompilerParams(vmem_limit_bytes=24 * 1024 * 1024),
        cost_estimate=pl.CostEstimate(flops=flops, bytes_accessed=size, transcendentals=0),
    )(*arrays)
    return out if len(shapes) > 1 else out[0]


def call_pack(ids, layer_input, out_grad):
    width, tokens = layer_input.shape
    return pl.pallas_call(
        pack_kernel,
        out_shape=jax.ShapeDtypeStruct((width + PAD, 2 * tokens), BF16),
        in_specs=[pl.BlockSpec(memory_space=pl.ANY)] * 3,
        out_specs=pl.BlockSpec(memory_space=pltpu.VMEM),
        scratch_shapes=[pltpu.VMEM(ids.shape, jnp.int32), pltpu.SemaphoreType.DMA((3,))],
        compiler_params=pltpu.CompilerParams(vmem_limit_bytes=60 * 1024 * 1024),
        cost_estimate=pl.CostEstimate(flops=0, bytes_accessed=8 * tokens * width, transcendentals=0),
    )(ids, layer_input, out_grad)


def shards(layer_input, out_grad, expert_ids, gate_probs, w_gate, w_up, w_down):
    groups = N_Z * N_X
    tokens, width = layer_input.shape
    rows = groups * SLOTS
    chip = N_C * width
    core = lax.axis_index("c")
    here = lax.axis_index("y")
    core_ref = core.astype(jnp.int32).reshape(1)

    both = lax.all_gather(call_pack(expert_ids.T, layer_input.T, out_grad.T), "c", axis=0, tiled=True)
    send = call(dispatch_kernel, [(groups, 2 * SLOTS, chip)], [core_ref, both], 8 * rows * chip * tokens)
    weights = call(weight_kernel, [(rows, 2 * tokens)], (core_ref, expert_ids.T, gate_probs.T), rows * tokens * 256)

    send, w_gate, w_up, w_down = lax.optimization_barrier((send, w_gate, w_up, w_down))
    recv = lax.all_to_all(send, ORDER, split_axis=0, concat_axis=0, tiled=True)

    mats = jnp.stack([w_gate[0], w_up[0], w_down[0].T])

    def part(step):
        return lax.dynamic_slice_in_dim(mats, chip * ((here + step) % N_Y), chip, axis=1)

    blocks = [part(0)] + [shift(part(d), "y", d, N_Y) for d in range(1, N_Y)]
    other_0, other_1, other_2, other_3 = (shift(block, "c", 1, N_C) for block in blocks)

    units = N_C * w_gate.shape[2]
    shape = (3, rows, units)
    product = 2 * rows * chip * units
    rows_in, rows_grad, part_2 = call(
        first_kernel, [(rows, chip), (rows, chip), shape], [recv, blocks[2], other_2], 3 * product
    )
    arrived = shift(part_2, "y", -2, N_Y)
    part_1 = call(next_kernel, [shape], [rows_in, rows_grad, blocks[1], other_1], 3 * product)
    part_1 = shift(part_1, "y", -1, N_Y)
    part_3 = call(next_kernel, [shape], [rows_in, rows_grad, blocks[3], other_3], 3 * product)
    part_3 = shift(part_3, "y", -3, N_Y)
    part_0 = call(own_kernel, [shape], [rows_in, rows_grad, blocks[0], other_0, arrived], 3 * product, F32)
    grads = call(hidden_kernel, [(2, rows, units)], [part_0, part_1, part_3], 40 * rows * units)
    grads_2, grads_1, grads_3 = (shift(grads, "y", d, N_Y) for d in (2, 1, 3))
    total = call(
        early_kernel, [(rows, chip)], [grads, grads_2, blocks[0], blocks[2], other_0, other_2], 4 * product, F32
    )
    back = call(
        back_kernel,
        [(groups, SLOTS, chip)],
        [total, grads_1, grads_3, blocks[1], blocks[3], other_1, other_3],
        4 * product,
    )
    returned = lax.all_to_all(back, ORDER, split_axis=0, concat_axis=0, tiled=True).reshape(rows, chip)
    mixed = dot(returned, weights, 0, 0)
    mixed = (mixed[:, :tokens] + mixed[:, tokens:]).reshape(N_C, width, tokens)
    mine = lax.dynamic_index_in_dim(mixed, core, 0, keepdims=False)
    sibling = lax.dynamic_index_in_dim(mixed, 1 - core, 0, keepdims=False)
    sent = lax.all_gather(sibling, "c", axis=0)
    result = mine + lax.dynamic_index_in_dim(sent, 1 - core, 0, keepdims=False)
    return result.astype(BF16).T


def solution(mesh):
    split = Mesh(mesh.devices.reshape(N_Z, N_X, N_Y, N_C), GROUP + LOCAL)
    placed = (
        P(GROUP, LOCAL),
        P(GROUP, LOCAL),
        P(GROUP, None),
        P(GROUP, None),
        P(GROUP, None, LOCAL),
        P(GROUP, None, LOCAL),
        P(GROUP, LOCAL, None),
    )
    return jax.shard_map(
        shards, mesh=split, in_specs=placed, out_specs=P(GROUP, LOCAL), check_vma=False
    )
```
